32 devices in a mesh: batch: 4 (over z), tm: 8 (over y, x, core).
Axes of the slice: x: 2, y: 2, z: 4, core: 2. Of those that a mesh axis runs over, the one named last changes fastest.
Arguments:
- frames: bfloat16 [16, 512, 512], P('batch', 'tm'), may hold values from -6 to 6
- noise: float32 [16, 32, 512], P('batch', None, 'tm'), may hold values from -4 to 7.5
- frame_lengths: int32 [16], P('batch'), may hold values from 64 to 512, as said below
- labels: int32 [16, 32], P('batch'), may hold values from 1 to 999
- label_lengths: int32 [16], P('batch'), may hold values from 16 to 32, as said below
- w_in: bfloat16 [512, 4096], P(None, ('batch', 'tm')), may hold values from -0.25 to 0.25
- w_rec: bfloat16 [1024, 4096], P(None, ('batch', 'tm')), may hold values from -0.1875 to 0.1875
- ln_gain: float32 [4096], replicated, may hold values from 0.5 to 1.5
- ln_shift: float32 [4096], replicated, may hold values from -1.5 to 1.5
- init_state: float32 [2, 1024], replicated, may hold values from -3 to 3
- dec_table: bfloat16 [1000, 4096], P(None, ('batch', 'tm')), may hold values from -3 to 3
- dec_rec: bfloat16 [1024, 4096], P(None, ('batch', 'tm')), may hold values from -0.1875 to 0.1875
- att_query: bfloat16 [1024, 2048], P(None, ('batch', 'tm')), may hold values from -0.1875 to 0.1875
- att_key: bfloat16 [1024, 2048], P(None, ('batch', 'tm')), may hold values from -0.1875 to 0.1875
- att_bias: float32 [2, 1024], replicated, may hold values from -1.5 to 1.5
- att_vec: float32 [2, 1024], replicated, may hold values from -0.5 to 0.5
- monotonic: float32 [2], replicated, may hold values from -7.5 to 2, as said below
- proj_w: bfloat16 [2048, 1024], P(None, ('batch', 'tm')), may hold values from -0.125 to 0.125
- proj_b: float32 [1024], replicated, may hold values from -1.5 to 1.5
- out_w: bfloat16 [1024, 1000], P(('batch', 'tm')), may hold values from -0.5 to 0.5
- out_b: float32 [1000], replicated, may hold values from -2.5 to 2.5
Outputs:
- loss: float32 [], replicated
- frames_grad: float32 [16, 512, 512], P('batch', 'tm')
- w_in_grad: float32 [512, 4096], P(None, ('batch', 'tm'))
- w_rec_grad: float32 [1024, 4096], P(None, ('batch', 'tm'))
- ln_gain_grad: float32 [4096], replicated
- ln_shift_grad: float32 [4096], replicated
- init_state_grad: float32 [2, 1024], replicated
- dec_table_grad: float32 [1000, 4096], P(None, ('batch', 'tm'))
- dec_rec_grad: float32 [1024, 4096], P(None, ('batch', 'tm'))
- att_query_grad: float32 [1024, 2048], P(None, ('batch', 'tm'))
- att_key_grad: float32 [1024, 2048], P(None, ('batch', 'tm'))
- att_bias_grad: float32 [2, 1024], replicated
- att_vec_grad: float32 [2, 1024], replicated
- monotonic_grad: float32 [2], replicated
- proj_w_grad: float32 [2048, 1024], P(None, ('batch', 'tm'))
- proj_b_grad: float32 [1024], replicated
- out_w_grad: float32 [1024, 1000], P(('batch', 'tm'))
- out_b_grad: float32 [1000], replicated
The draws below stay inside these ranges and needn't reach their ends.
Inputs may be any that keep to these rules, and one draw needn't show every extreme that they name: `frame_lengths`: in every aligned block of 4 utterances one has all 512 frames. `label_lengths`: in every aligned block of 4 utterances one has all 32 labels. `labels`: label 0 is the start symbol and is never a target. `monotonic`: the first entry is g, the second r.
All inputs are finite; a program needn't handle non-finite values.
Results may differ from the reference program's by a relative error of at most 0.014.
Values may be sent and summed in bfloat16 or wider, within the bound.
No kernel may reach another device: no remote copies, remote signals or barrier semaphores. Data moves between devices by JAX's collectives and lax.ppermute only.
A program may use at most 256 MiB of HBM per device.

```python
import jax
import jax.numpy as jnp
from jax import lax

HID = 1024
FEAT = 512
ATT = 1024
PROJ = 1024
VOCAB = 1000
BLOCK = 16
FRAME_DEV = 64
UTT_DEV = 4
OUTPUT_TOKENS = 32
AUDIO_SLICES = 512
SPEECH_SAMPLES = 16
N_TM = 8


def full_one_per_group(key, lowest, highest_value):
    first_key, pick_key = jax.random.split(key)
    lengths = jax.random.randint(first_key, (SPEECH_SAMPLES,), lowest, highest_value + 1)
    chosen_slot = jax.random.randint(pick_key, (SPEECH_SAMPLES // UTT_DEV,), 0, UTT_DEV)
    slot_index = jnp.arange(SPEECH_SAMPLES) % UTT_DEV
    group_index = jnp.arange(SPEECH_SAMPLES) // UTT_DEV
    chosen = slot_index == chosen_slot[group_index]
    return jnp.where(chosen, highest_value, lengths).astype(jnp.int32)


def draw_frame_lengths(key, part):
    return full_one_per_group(jax.random.fold_in(key, 11), AUDIO_SLICES // 8, AUDIO_SLICES)


def draw_label_lengths(key, part):
    return full_one_per_group(jax.random.fold_in(key, 23), OUTPUT_TOKENS // 2, OUTPUT_TOKENS)


def draw_monotonic(key, part):
    gain_key, offset_key = jax.random.split(key)
    gain_value = jax.random.uniform(gain_key, (1,), jnp.float32, 1.0, 2.0)
    offset_value = jax.random.uniform(offset_key, (1,), jnp.float32, -7.5, -6.0)
    return jnp.concatenate([gain_value, offset_value])


def draw_noise(key, part):
    key = jax.random.fold_in(key, 37)
    base_key, spot_key = jax.random.split(key)
    starting_index = jnp.clip(jax.random.normal(base_key, (SPEECH_SAMPLES, OUTPUT_TOKENS, AUDIO_SLICES), jnp.float32), -4.0, 4.0)
    chosen_place = jax.random.randint(spot_key, (SPEECH_SAMPLES, OUTPUT_TOKENS, N_TM), 0, FRAME_DEV)
    shard_entries = jnp.arange(FRAME_DEV)
    transfer_extent = (shard_entries[None, None, None, :] == chosen_place[..., None]).astype(jnp.float32)
    transfer_extent = transfer_extent.reshape(SPEECH_SAMPLES, OUTPUT_TOKENS, AUDIO_SLICES)
    return starting_index + 3.5 * transfer_extent


def plant(entries, own_key, least, high):
    longest = entries.shape.index(max(entries.shape))
    spots = []
    for shift in (0, 1):
        where = [jax.random.randint(jax.random.fold_in(own_key, axis), (), 0, length) for axis, length in enumerate(entries.shape)]
        where[longest] = (where[longest] + shift) % entries.shape[longest]
        spots.append(tuple(where))
    return entries.at[spots[0]].set(least).at[spots[1]].set(high)


def levels(key, shape, shards, low, top_value):
    level, own = 1.0, jax.random.fold_in(key, 6)
    for position, blocks in shards:
        heights = jnp.exp(jax.random.uniform(jax.random.fold_in(own, position), (blocks,), jnp.float32, low / len(shards), top_value / len(shards)))
        level = level * jnp.repeat(heights, shape[position] // blocks).reshape([-1 if axis == position else 1 for axis in range(len(shape))])
    return level


def normal_values(own_key, shape, scale, limit, shards=(), held_as=jnp.bfloat16):
    values = jax.random.normal(own_key, shape, jnp.float32) * scale
    if len(shards) > 0:
        values = levels(own_key, shape, shards, -0.22, 0.18) * values
    return jnp.clip(values, min=-limit, max=limit).astype(held_as)


def setup_inputs(seed: int = 0) -> dict:
    splits = jax.random.split(jax.random.key(seed), 22)
    frames = normal_values(splits[0], (SPEECH_SAMPLES, AUDIO_SLICES, FEAT), 1.0, 6.0, ((0, 4), (1, 8)))
    noise = draw_noise(jax.random.fold_in(splits[21], 71), 0)
    frame_lengths = draw_frame_lengths(jax.random.fold_in(splits[21], 71), 0)
    labels = plant(jax.random.randint(splits[3], (SPEECH_SAMPLES, OUTPUT_TOKENS), 1, VOCAB), jax.random.fold_in(splits[3], 1), 1, VOCAB - 1).astype(jnp.int32)
    label_lengths = draw_label_lengths(jax.random.fold_in(splits[21], 71), 0)
    w_in = normal_values(splits[5], (FEAT, 4 * HID), FEAT ** -0.5, 0.25, ((1, 32),))
    w_rec = normal_values(splits[6], (HID, 4 * HID), HID ** -0.5, 0.1875, ((1, 32),))
    ln_gain = jnp.clip(1.0 + 0.1 * jax.random.normal(splits[7], (4 * HID,), jnp.float32), 0.5, 1.5)
    ln_shift = normal_values(splits[8], (4 * HID,), 0.3, 1.5, (), jnp.float32)
    init_state = normal_values(splits[9], (2, HID), 0.5, 3.0, (), jnp.float32)
    dec_table = normal_values(splits[10], (VOCAB, 4 * HID), 0.5, 3.0, ((1, 32),))
    dec_rec = normal_values(splits[11], (HID, 4 * HID), HID ** -0.5, 0.1875, ((1, 32),))
    att_query = normal_values(splits[12], (HID, 2 * ATT), HID ** -0.5, 0.1875, ((1, 32),))
    att_key = normal_values(splits[13], (HID, 2 * ATT), HID ** -0.5, 0.1875, ((1, 32),))
    att_bias = normal_values(splits[14], (2, ATT), 0.3, 1.5, (), jnp.float32)
    att_vec = normal_values(splits[15], (2, ATT), 0.1, 0.5, (), jnp.float32)
    monotonic = draw_monotonic(jax.random.fold_in(splits[21], 71), 0)
    proj_w = normal_values(splits[17], (2 * HID, PROJ), (2 * HID) ** -0.5, 0.125, ((1, 32),))
    proj_b = normal_values(splits[18], (PROJ,), 0.3, 1.5, (), jnp.float32)
    out_w = normal_values(splits[19], (PROJ, VOCAB), (PROJ // 8) ** -0.5, 0.5, ((0, 32),))
    out_b = normal_values(splits[20], (VOCAB,), 0.5, 2.5, (), jnp.float32)
    return {"frames": frames, "noise": noise, "frame_lengths": frame_lengths, "labels": labels, "label_lengths": label_lengths, "w_in": w_in, "w_rec": w_rec, "ln_gain": ln_gain, "ln_shift": ln_shift, "init_state": init_state, "dec_table": dec_table, "dec_rec": dec_rec, "att_query": att_query, "att_key": att_key, "att_bias": att_bias, "att_vec": att_vec, "monotonic": monotonic, "proj_w": proj_w, "proj_b": proj_b, "out_w": out_w, "out_b": out_b}


@jax.custom_vjp
def low(v):
    return lax.optimization_barrier(v.astype(jnp.bfloat16)).astype(jnp.float32)

@jax.custom_vjp
def low_back(v):
    return v

def low_keep(v):
    return (low(v), None)

def low_pass(kept, grad):
    return (grad,)

def back_keep(v):
    return (v, None)

def back_low(kept, grad):
    return (low(grad),)
low.defvjp(low_keep, low_pass)
low_back.defvjp(back_keep, back_low)
highest = lax.Precision.HIGHEST
norm_eps = 1e-05

def matmul(left, right):
    return jnp.dot(left, right, precision=highest, preferred_element_type=jnp.float32)

def plain_cell(gate_vals, cell_state):
    in_gate, forget, candidate, out_gate = jnp.split(gate_vals, 4, axis=-1)
    new_cell = jax.nn.sigmoid(forget) * cell_state + jax.nn.sigmoid(in_gate) * jnp.tanh(candidate)
    return (jax.nn.sigmoid(out_gate) * jnp.tanh(new_cell), new_cell)

def norm_cell(preact, cell_state, gain, shift):
    row_mean = lax.optimization_barrier(jnp.mean(preact, axis=-1, keepdims=True))
    centred = preact - row_mean
    row_var = lax.optimization_barrier(jnp.mean(centred * centred, axis=-1, keepdims=True))
    gate_vals = centred * lax.rsqrt(row_var + norm_eps) * gain + shift
    return plain_cell(gate_vals, cell_state)

def energy_terms(queries, key_proj, att_bias, att_vec, monotonic):
    width = queries.shape[-1] // 2
    mono_act = jnp.tanh(queries[:, None, :width] + key_proj[None, :, :width] + att_bias[0])
    span_act = jnp.tanh(queries[:, None, width:] + key_proj[None, :, width:] + att_bias[1])
    vec_scale = monotonic[0] * lax.rsqrt(jnp.sum(att_vec[0] * att_vec[0]) + 1e-06)
    mono_energy = lax.optimization_barrier(jnp.sum(mono_act * att_vec[0], axis=-1)) * vec_scale + monotonic[1]
    span_energy = lax.optimization_barrier(jnp.sum(span_act * att_vec[1], axis=-1))
    return (mono_energy, span_energy)

def utterance(params, frames, noise, frame_length, label_row, label_length):
    w_in, w_rec, ln_gain, ln_shift, init_state, dec_table, dec_rec, att_query, att_key, att_bias, att_vec, monotonic, proj_w, proj_b, out_w, out_b = params
    block_count = AUDIO_SLICES // BLOCK
    step_in = low_back(matmul(frames, w_in)).reshape(block_count, BLOCK, 4 * HID)
    start_hidden = jnp.broadcast_to(low(init_state[0]), (block_count, HID))
    start_cell = jnp.broadcast_to(init_state[1], (block_count, HID))

    def enc_step(state_carry, step_input):
        prev_hidden, prev_cell = state_carry
        preact = step_input + low_back(matmul(prev_hidden, w_rec))
        new_hidden, new_cell = norm_cell(preact, prev_cell, ln_gain, ln_shift)
        new_hidden = low(new_hidden)
        return ((new_hidden, new_cell), new_hidden)
    final_state, enc_out = lax.scan(enc_step, (start_hidden, start_cell), jnp.swapaxes(step_in, 0, 1))
    memory = jnp.swapaxes(enc_out, 0, 1).reshape(AUDIO_SLICES, HID)
    key_proj = low_back(matmul(memory, att_key))
    prev_ids = jnp.concatenate([jnp.zeros((1,), jnp.int32), label_row[:-1].astype(jnp.int32)])
    table_rows = dec_table[prev_ids]
    zero_state = jnp.zeros((HID,), jnp.float32)

    def dec_step(state_carry, table_row):
        prev_state, prev_cell = state_carry
        preact = table_row + low_back(matmul(prev_state, dec_rec))
        new_state, new_cell = plain_cell(preact, prev_cell)
        new_state = low(new_state)
        return ((new_state, new_cell), new_state)
    dec_final, states = lax.scan(dec_step, (zero_state, zero_state), table_rows)
    queries = low_back(matmul(states, att_query))

    def energy_block(key_block):
        return energy_terms(queries, key_block, att_bias, att_vec, monotonic)
    mono_blocks, span_blocks = lax.map(jax.checkpoint(energy_block), key_proj.reshape(N_TM, FRAME_DEV, 2 * ATT))
    mono_energy = jnp.moveaxis(mono_blocks, 0, 1).reshape(OUTPUT_TOKENS, AUDIO_SLICES)
    span_energy = jnp.moveaxis(span_blocks, 0, 1).reshape(OUTPUT_TOKENS, AUDIO_SLICES)
    energy = mono_energy + noise
    frame_mask = (jnp.arange(AUDIO_SLICES) < frame_length).astype(jnp.float32)
    stop_prob = jax.nn.sigmoid(energy) * frame_mask
    survive = jnp.cumprod(1.0 - stop_prob, axis=1)
    ones_column = jnp.ones((OUTPUT_TOKENS, 1), jnp.float32)
    zero_column = jnp.zeros((OUTPUT_TOKENS, 1), jnp.float32)
    before = jnp.concatenate([ones_column, survive[:, :-1]], axis=1)
    alignment = stop_prob * before
    self_share = jnp.concatenate([ones_column, jax.nn.sigmoid(span_energy[:, 1:] - span_energy[:, :-1])], axis=1)
    next_align = jnp.concatenate([alignment[:, 1:], zero_column], axis=1)
    next_share = jnp.concatenate([self_share[:, 1:], ones_column], axis=1)
    span_weight = alignment * self_share + next_align * (1.0 - next_share)
    context = matmul(low(span_weight), memory)
    joined = jnp.concatenate([states, low(low_back(context))], axis=-1)
    proj_out = jnp.tanh(low_back(matmul(joined, proj_w)) + proj_b)
    logits = low_back(matmul(low(proj_out), out_w)) + out_b
    log_norm = jax.nn.logsumexp(logits, axis=-1)
    picked = jnp.take_along_axis(logits, label_row[:, None].astype(jnp.int32), axis=-1)[:, 0]
    label_mask = (jnp.arange(OUTPUT_TOKENS) < label_length).astype(jnp.float32)
    return jnp.sum((log_norm - picked) * label_mask)

def reference(frames, noise, frame_lengths, labels, label_lengths, w_in, w_rec, ln_gain, ln_shift, init_state, dec_table, dec_rec, att_query, att_key, att_bias, att_vec, monotonic, proj_w, proj_b, out_w, out_b):
    params = tuple((array_in.astype(jnp.float32) for array_in in (w_in, w_rec, ln_gain, ln_shift, init_state, dec_table, dec_rec, att_query, att_key, att_bias, att_vec, monotonic, proj_w, proj_b, out_w, out_b)))

    def total(param_set, frames_float):

        def single(packed):
            return utterance(param_set, packed[0], packed[1], packed[2], packed[3], packed[4])
        losses = lax.map(jax.checkpoint(single), (frames_float, noise, frame_lengths, labels, label_lengths))
        return jnp.sum(losses)
    loss_sum, pullback = jax.vjp(total, params, frames.astype(jnp.float32))
    param_grads, frame_grad = pullback(jnp.ones((), jnp.float32))
    return (loss_sum, frame_grad, param_grads[0], param_grads[1], param_grads[2], param_grads[3], param_grads[4], param_grads[5], param_grads[6], param_grads[7], param_grads[8], param_grads[9], param_grads[10], param_grads[11], param_grads[12], param_grads[13], param_grads[14], param_grads[15])
```

```python
import functools

import jax
import jax.numpy as jnp
from jax import lax
from jax.experimental import pallas as pl
from jax.experimental.pallas import tpu as pltpu
from jax.sharding import Mesh
from jax.sharding import PartitionSpec as P

BLOCK = 16
LANES = 128
norm_eps = 1e-05
f32 = jnp.float32
bf16 = jnp.bfloat16
CHIPS = ("batch", "chip")
ALL = ("batch", "chip", "core")
VMEM_LIMIT = 60 * 2**20


def sigmoid(v):
    return 0.5 * jnp.tanh(0.5 * v) + 0.5


def forward_dot(left, right):
    return jnp.dot(left, right, preferred_element_type=f32)


def dot_last(left, right):
    return lax.dot_general(left, right, (((left.ndim - 1,), (1,)), ((), ())), preferred_element_type=f32)


def dot_first(left, right):
    return lax.dot_general(left, right, (((0,), (0,)), ((), ())), preferred_element_type=f32)


def params():
    return pltpu.CompilerParams(vmem_limit_bytes=VMEM_LIMIT)


def whole(count, smem_first=True):
    specs = [pl.BlockSpec(memory_space=pltpu.VMEM)] * count
    if smem_first:
        specs[0] = pl.BlockSpec(memory_space=pltpu.SMEM)
    return specs


def dec_forward_kernel(core_ref, table_ref, weight_ref, state_ref, gate_ref, cell_ref):
    steps, hidden = state_ref.shape

    @pl.when(core_ref[0] == 1)
    def _():
        def step(index, carry):
            prev_state, prev_cell = carry
            preact = table_ref[pl.ds(index, 1), :] + forward_dot(prev_state, weight_ref[...])[0:1]
            in_gate = sigmoid(preact[:, :hidden])
            forget = sigmoid(preact[:, hidden : 2 * hidden])
            candidate = jnp.tanh(preact[:, 2 * hidden : 3 * hidden])
            out_gate = sigmoid(preact[:, 3 * hidden :])
            cell = forget * prev_cell + in_gate * candidate
            state = out_gate * jnp.tanh(cell)
            gate_ref[pl.ds(index, 1), :hidden] = in_gate
            gate_ref[pl.ds(index, 1), hidden : 2 * hidden] = forget
            gate_ref[pl.ds(index, 1), 2 * hidden : 3 * hidden] = candidate
            gate_ref[pl.ds(index, 1), 3 * hidden :] = out_gate
            cell_ref[pl.ds(index, 1), :] = cell
            state_ref[pl.ds(index, 1), :] = state
            return (jnp.broadcast_to(state, (16, hidden)).astype(bf16), cell)

        lax.fori_loop(
            0, steps, step, (jnp.zeros((16, hidden), bf16), jnp.zeros((1, hidden), f32))
        )

    @pl.when(core_ref[0] != 1)
    def _():
        state_ref[...] = jnp.zeros_like(state_ref)
        gate_ref[...] = jnp.zeros_like(gate_ref)
        cell_ref[...] = jnp.zeros_like(cell_ref)


def dec_forward(core, table_rows, weight):
    steps, width = table_rows.shape
    hidden = width // 4
    return pl.pallas_call(
        dec_forward_kernel,
        in_specs=whole(3),
        out_shape=[
            jax.ShapeDtypeStruct((steps, hidden), f32),
            jax.ShapeDtypeStruct((steps, width), f32),
            jax.ShapeDtypeStruct((steps, hidden), f32),
        ],
        compiler_params=params(),
        name="dec_forward",
    )(core, table_rows, weight)


def transpose_into(target_ref, weight_ref):
    width = weight_ref.shape[1]

    def part(index, carry):
        start = pl.multiple_of(index * 256, 256)
        target_ref[pl.ds(start, 256), :] = weight_ref[:, pl.ds(start, 256)].T
        return carry

    lax.fori_loop(0, width // 256, part, 0)


def dec_backward_kernel(core_ref, gate_ref, cell_ref, grad_ref, weight_ref, out_ref, turned_ref):
    steps, hidden = grad_ref.shape

    @pl.when(core_ref[0] == 1)
    def _():
        transpose_into(turned_ref, weight_ref)

        def step(back, carry):
            rec_grad, cell_grad = carry
            index = steps - 1 - back
            row = pl.ds(index, 1)
            in_gate = gate_ref[row, :hidden]
            forget = gate_ref[row, hidden : 2 * hidden]
            candidate = gate_ref[row, 2 * hidden : 3 * hidden]
            out_gate = gate_ref[row, 3 * hidden :]
            prev_cell = jnp.where(index > 0, cell_ref[pl.ds(jnp.maximum(index - 1, 0), 1), :], 0.0)
            squashed = jnp.tanh(cell_ref[row, :])
            state_grad = grad_ref[row, :] + rec_grad
            cell_grad = cell_grad + state_grad * out_gate * (1.0 - squashed * squashed)
            pre_grad = jnp.concatenate(
                [
                    cell_grad * candidate * in_gate * (1.0 - in_gate),
                    cell_grad * prev_cell * forget * (1.0 - forget),
                    cell_grad * in_gate * (1.0 - candidate * candidate),
                    state_grad * squashed * out_gate * (1.0 - out_gate),
                ],
                axis=1,
            )
            out_ref[row, :] = pre_grad
            low = jnp.broadcast_to(pre_grad, (16, 4 * hidden)).astype(bf16)
            return (forward_dot(low, turned_ref[...])[0:1], cell_grad * forget)

        zero = jnp.zeros((1, hidden), f32)
        lax.fori_loop(0, steps, step, (zero, zero))

    @pl.when(core_ref[0] != 1)
    def _():
        out_ref[...] = jnp.zeros_like(out_ref)


def dec_backward(core, gates, cells, state_grad, weight):
    steps, hidden = state_grad.shape
    return pl.pallas_call(
        dec_backward_kernel,
        in_specs=whole(5),
        out_shape=jax.ShapeDtypeStruct((steps, 4 * hidden), f32),
        scratch_shapes=[pltpu.VMEM((4 * hidden, hidden), bf16)],
        compiler_params=params(),
        name="dec_backward",
    )(core, gates, cells, state_grad, weight)


def enc_forward_kernel(
    core_ref,
    frame_ref,
    in_ref,
    weight_ref,
    gain_ref,
    shift_ref,
    init_ref,
    hidden_ref,
    norm_ref,
    cell_ref,
    scale_ref,
):
    steps, rows, hidden = hidden_ref.shape
    width = 4 * hidden

    @pl.when(core_ref[0] == 0)
    def _():
        def feed(index, carry):
            columns = pl.ds(pl.multiple_of(index * 512, 512), 512)
            part = forward_dot(frame_ref[...], in_ref[:, columns])
            norm_ref[:, :, columns] = part.reshape(steps, rows, 512)
            return carry

        lax.fori_loop(0, width // 512, feed, 0)

        def step(index, carry):
            prev_hidden, prev_cell = carry
            preact = norm_ref[index] + forward_dot(prev_hidden, weight_ref[...])
            centred = preact - jnp.mean(preact, axis=-1, keepdims=True)
            scale = lax.rsqrt(jnp.mean(centred * centred, axis=-1, keepdims=True) + norm_eps)
            normed = centred * scale
            norm_ref[index] = normed
            scale_ref[index] = jnp.broadcast_to(scale, (rows, LANES))

            def gate(which):
                columns = slice(which * hidden, (which + 1) * hidden)
                return normed[:, columns] * gain_ref[:, columns] + shift_ref[:, columns]

            cell = sigmoid(gate(1)) * prev_cell + sigmoid(gate(0)) * jnp.tanh(gate(2))
            state = (sigmoid(gate(3)) * jnp.tanh(cell)).astype(bf16)
            cell_ref[index] = cell
            hidden_ref[index] = state
            return (state, cell)

        start = (
            jnp.broadcast_to(init_ref[0:1, :], (rows, hidden)).astype(bf16),
            jnp.broadcast_to(init_ref[1:2, :], (rows, hidden)),
        )
        lax.fori_loop(0, steps, step, start)

    @pl.when(core_ref[0] != 0)
    def _():
        hidden_ref[...] = jnp.zeros_like(hidden_ref)


def enc_forward(core, frame_rows, w_in, w_rec, gain, shift, init_state):
    hidden = w_rec.shape[0]
    steps, rows = BLOCK, frame_rows.shape[0] // BLOCK
    return pl.pallas_call(
        enc_forward_kernel,
        in_specs=whole(7),
        out_shape=[
            jax.ShapeDtypeStruct((steps, rows, hidden), bf16),
            jax.ShapeDtypeStruct((steps, rows, 4 * hidden), f32),
            jax.ShapeDtypeStruct((steps, rows, hidden), f32),
            jax.ShapeDtypeStruct((steps, rows, LANES), f32),
        ],
        compiler_params=params(),
        name="enc_forward",
    )(core, frame_rows, w_in, w_rec, gain, shift, init_state)


def enc_backward_kernel(
    core_ref,
    norm_ref,
    cell_ref,
    scale_ref,
    grad_ref,
    weight_ref,
    gain_ref,
    shift_ref,
    init_ref,
    out_ref,
    gain_grad_ref,
    shift_grad_ref,
    init_grad_ref,
    turned_ref,
    gain_sum,
    shift_sum,
):
    steps, rows, hidden = grad_ref.shape
    width = 4 * hidden

    @pl.when(core_ref[0] == 0)
    def _():
        transpose_into(turned_ref, weight_ref)
        gain_sum[...] = jnp.zeros_like(gain_sum)
        shift_sum[...] = jnp.zeros_like(shift_sum)

        def step(back, carry):
            rec_grad, cell_grad = carry
            index = steps - 1 - back

            def gate(which):
                columns = slice(which * hidden, (which + 1) * hidden)
                return norm_ref[index, :, columns] * gain_ref[:, columns] + shift_ref[:, columns]

            in_gate, forget = (sigmoid(gate(0)), sigmoid(gate(1)))
            candidate, out_gate = (jnp.tanh(gate(2)), sigmoid(gate(3)))
            start_cell = jnp.broadcast_to(init_ref[1:2, :], (rows, hidden))
            prev_cell = jnp.where(index > 0, cell_ref[jnp.maximum(index - 1, 0)], start_cell)
            squashed = jnp.tanh(cell_ref[index])
            state_grad = grad_ref[index] + rec_grad
            cell_grad = cell_grad + state_grad * out_gate * (1.0 - squashed * squashed)
            gate_grad = jnp.concatenate(
                [
                    cell_grad * candidate * in_gate * (1.0 - in_gate),
                    cell_grad * prev_cell * forget * (1.0 - forget),
                    cell_grad * in_gate * (1.0 - candidate * candidate),
                    state_grad * squashed * out_gate * (1.0 - out_gate),
                ],
                axis=1,
            )
            normed = norm_ref[index]
            gain_sum[...] += jnp.sum((gate_grad * normed).reshape(rows // 8, 8, width), axis=0)
            shift_sum[...] += jnp.sum(gate_grad.reshape(rows // 8, 8, width), axis=0)
            scaled = gate_grad * gain_ref[...]
            mean_grad = jnp.mean(scaled, axis=-1, keepdims=True)
            mean_normed = jnp.mean(scaled * normed, axis=-1, keepdims=True)
            pre_grad = scale_ref[index, :, 0:1] * (scaled - mean_grad - normed * mean_normed)
            low = pre_grad.astype(bf16)
            out_ref[index] = low
            return (forward_dot(low, turned_ref[...]), cell_grad * forget)

        zero = jnp.zeros((rows, hidden), f32)
        hidden_grad, cell_grad = lax.fori_loop(0, steps, step, (zero, zero))
        gain_grad_ref[...] = jnp.sum(gain_sum[...], axis=0, keepdims=True)
        shift_grad_ref[...] = jnp.sum(shift_sum[...], axis=0, keepdims=True)
        init_grad_ref[0:1, :] = jnp.sum(hidden_grad, axis=0, keepdims=True)
        init_grad_ref[1:2, :] = jnp.sum(cell_grad, axis=0, keepdims=True)

    @pl.when(core_ref[0] != 0)
    def _():
        out_ref[...] = jnp.zeros_like(out_ref)
        gain_grad_ref[...] = jnp.zeros_like(gain_grad_ref)
        shift_grad_ref[...] = jnp.zeros_like(shift_grad_ref)
        init_grad_ref[...] = jnp.zeros_like(init_grad_ref)


def enc_backward(core, normed, cells, scales, memory_grad, w_rec, gain, shift, init_state):
    steps, rows, hidden = memory_grad.shape
    return pl.pallas_call(
        enc_backward_kernel,
        in_specs=whole(9),
        out_shape=[
            jax.ShapeDtypeStruct((steps, rows, 4 * hidden), bf16),
            jax.ShapeDtypeStruct((1, 4 * hidden), f32),
            jax.ShapeDtypeStruct((1, 4 * hidden), f32),
            jax.ShapeDtypeStruct((2, hidden), f32),
        ],
        scratch_shapes=[
            pltpu.VMEM((4 * hidden, hidden), bf16),
            pltpu.VMEM((8, 4 * hidden), f32),
            pltpu.VMEM((8, 4 * hidden), f32),
        ],
        compiler_params=params(),
        name="enc_backward",
    )(core, normed, cells, scales, memory_grad, w_rec, gain, shift, init_state)


def moved(value, by, fill):
    count = value.shape[1]
    lane = lax.broadcasted_iota(jnp.int32, value.shape, 1)
    rolled = pltpu.roll(value, by % count, 1)
    inside = lane >= by if by > 0 else lane < count + by
    return jnp.where(inside, rolled, fill)


def spans(count):
    sizes, size = ([], 1)
    while size < count:
        sizes.append(size)
        size *= 2
    return sizes


def attend_kernel(
    scalar_ref,
    length_ref,
    query_ref,
    key_ref,
    vec_ref,
    noise_ref,
    memory_ref,
    raw_ref,
    sig_ref,
    before_ref,
    align_ref,
    share_ref,
    weight_ref,
    context_ref,
    column_ref,
):
    steps, count = noise_ref.shape
    half = vec_ref.shape[1]
    lane = lax.broadcasted_iota(jnp.int32, (64, LANES), 1)

    def rows_loop(block, carry):
        rows = pl.ds(pl.multiple_of(block * 64, 64), 64)
        found = jnp.zeros((64, LANES), f32)
        for kind in range(2):

            def one(index, found):
                total = jnp.zeros((64, LANES), f32)
                for tile in range(half // LANES):
                    columns = pl.ds(kind * half + tile * LANES, LANES)
                    act = jnp.tanh(key_ref[rows, columns] + query_ref[index, :, columns])
                    total += act * vec_ref[kind : kind + 1, pl.ds(tile * LANES, LANES)]
                energy = jnp.sum(total, axis=1, keepdims=True)
                return jnp.where(lane == kind * steps + index, energy, found)

            found = lax.fori_loop(0, steps, one, found)
        column_ref[rows, :] = found
        return carry

    lax.fori_loop(0, count // 64, rows_loop, 0)
    energies = column_ref[...].T
    raw = energies[:steps]
    span = energies[steps : 2 * steps]
    position = lax.broadcasted_iota(jnp.int32, (steps, count), 1)
    mask = (position < length_ref[0]).astype(f32)
    sig = sigmoid(raw * scalar_ref[0] + scalar_ref[1] + noise_ref[...])
    stop = sig * mask
    survive = 1.0 - stop
    for size in spans(count):
        survive = survive * moved(survive, size, 1.0)
    before = moved(survive, 1, 1.0)
    align = stop * before
    share = jnp.where(position == 0, 1.0, sigmoid(span - moved(span, 1, 0.0)))
    weight = align * share + moved(align, -1, 0.0) * (1.0 - moved(share, -1, 1.0))
    raw_ref[...] = raw
    sig_ref[...] = sig
    before_ref[...] = before
    align_ref[...] = align
    share_ref[...] = share
    low = weight.astype(bf16)
    weight_ref[...] = low
    context_ref[...] = forward_dot(low, memory_ref[...]).astype(bf16)


def attend(scalars, length, queries, keys, att_vec, noise, memory):
    steps, count = noise.shape
    grid = jax.ShapeDtypeStruct((steps, count), f32)
    specs = whole(7)
    specs[1] = pl.BlockSpec(memory_space=pltpu.SMEM)
    return pl.pallas_call(
        attend_kernel,
        in_specs=specs,
        out_shape=[grid] * 5
        + [
            jax.ShapeDtypeStruct((steps, count), bf16),
            jax.ShapeDtypeStruct((steps, memory.shape[1]), bf16),
        ],
        scratch_shapes=[pltpu.VMEM((count, LANES), f32)],
        compiler_params=params(),
        name="attend",
    )(scalars, length, queries[:, None, :], keys, att_vec, noise, memory)


def attend_back_kernel(
    scalar_ref,
    length_ref,
    grad_ref,
    memory_ref,
    raw_ref,
    sig_ref,
    before_ref,
    align_ref,
    share_ref,
    query_ref,
    key_ref,
    vec_ref,
    key_grad_ref,
    query_grad_ref,
    vec_grad_ref,
    mono_ref,
    wide_ref,
    query_sum,
    vec_sum,
):
    steps, count = raw_ref.shape
    half = vec_ref.shape[1]
    position = lax.broadcasted_iota(jnp.int32, (steps, count), 1)
    mask = (position < length_ref[0]).astype(f32)
    sig, before, align, share = (sig_ref[...], before_ref[...], align_ref[...], share_ref[...])
    stop = sig * mask
    weight_grad = dot_last(grad_ref[...], memory_ref[...])
    prev_grad = moved(weight_grad, 1, 0.0)
    align_grad = weight_grad * share + prev_grad * (1.0 - share)
    term = align * (weight_grad - prev_grad) * share * (1.0 - share)
    span_grad = term - moved(term, -1, 0.0)
    later = align_grad * stop
    keep = 1.0 - stop
    for size in spans(count):
        later = later + keep * moved(later, -size, 0.0)
        keep = keep * moved(keep, -size, 1.0)
    stop_grad = before * (align_grad - moved(later, -1, 0.0))
    energy_grad = stop_grad * sig * (1.0 - sig) * mask
    raw_grad = energy_grad * scalar_ref[0]
    gain_part = jnp.sum(jnp.sum(energy_grad * raw_ref[...], axis=1, keepdims=True), axis=0, keepdims=True)
    shift_part = jnp.sum(jnp.sum(energy_grad, axis=1, keepdims=True), axis=0, keepdims=True)
    spot = lax.broadcasted_iota(jnp.int32, (1, LANES), 1)
    mono_ref[...] = jnp.where(spot == 0, gain_part, jnp.where(spot == 1, shift_part, 0.0))
    padding = jnp.zeros((LANES - 2 * steps, count), f32)
    columns_of = jnp.concatenate([raw_grad, span_grad, padding], axis=0).T
    for which in range(2 * steps):
        wide_ref[which] = jnp.broadcast_to(columns_of[:, which : which + 1], (count, LANES))
    query_sum[...] = jnp.zeros_like(query_sum)
    for kind in range(2):

        def tile_loop(tile, carry):
            columns = pl.ds(pl.multiple_of(kind * half + tile * LANES, LANES), LANES)
            vec_columns = pl.ds(pl.multiple_of(tile * LANES, LANES), LANES)
            vec = vec_ref[kind : kind + 1, vec_columns]

            def rows_loop(block, vec_part):
                rows = pl.ds(pl.multiple_of(block * 64, 64), 64)
                keys = key_ref[rows, columns]

                def one(index, carry):
                    key_part, vec_part = carry
                    act = jnp.tanh(keys + query_ref[index, :, columns])
                    wide = wide_ref[kind * steps + index, rows, :]
                    product = wide * act
                    slope = wide - product * act
                    folded = jnp.sum(slope.reshape(8, 8, LANES), axis=0)
                    query_sum[index, :, columns] += folded
                    return (key_part + slope, vec_part + jnp.sum(product.reshape(8, 8, LANES), axis=0))

                key_part, vec_part = lax.fori_loop(
                    0, steps, one, (jnp.zeros((64, LANES), f32), vec_part), unroll=2
                )
                key_grad_ref[rows, columns] = (key_part * vec).astype(bf16)
                return vec_part

            vec_part = lax.fori_loop(0, count // 64, rows_loop, jnp.zeros((8, LANES), f32))
            vec_sum[:, columns] = vec_part
            return carry

        lax.fori_loop(0, half // LANES, tile_loop, 0)
        vec_grad_ref[kind : kind + 1, :] = jnp.sum(
            vec_sum[:, kind * half : (kind + 1) * half], axis=0, keepdims=True
        )
    for index in range(steps):
        total = jnp.sum(query_sum[index], axis=0, keepdims=True)
        for kind in range(2):
            columns = slice(kind * half, (kind + 1) * half)
            query_grad_ref[index : index + 1, columns] = total[:, columns] * vec_ref[kind : kind + 1, :]


def attend_back(scalars, length, context_grad, memory, saved, queries, keys, att_vec):
    steps, count = saved[0].shape
    width = queries.shape[1]
    specs = whole(12)
    specs[1] = pl.BlockSpec(memory_space=pltpu.SMEM)
    return pl.pallas_call(
        attend_back_kernel,
        in_specs=specs,
        out_shape=[
            jax.ShapeDtypeStruct((count, width), bf16),
            jax.ShapeDtypeStruct((steps, width), f32),
            jax.ShapeDtypeStruct((2, width // 2), f32),
            jax.ShapeDtypeStruct((1, LANES), f32),
        ],
        scratch_shapes=[
            pltpu.VMEM((2 * steps, count, LANES), f32),
            pltpu.VMEM((steps, 8, width), f32),
            pltpu.VMEM((8, width), f32),
        ],
        compiler_params=params(),
        name="attend_back",
    )(scalars, length, context_grad, memory, *saved, queries[:, None, :], keys, att_vec)


def head_kernel(
    state_ref,
    context_ref,
    label_ref,
    mask_ref,
    proj_ref,
    proj_b_ref,
    out_w_ref,
    out_b_ref,
    loss_ref,
    out_b_grad_ref,
    proj_b_grad_ref,
    proj_low_ref,
    logit_low_ref,
    proj_grad_ref,
    state_grad_ref,
    context_grad_ref,
):
    hidden = state_ref.shape[1]
    rows, vocab = logit_low_ref.shape
    proj_out = jnp.tanh(
        forward_dot(state_ref[...], proj_ref[:hidden, :])
        + forward_dot(context_ref[...], proj_ref[hidden:, :])
        + proj_b_ref[...]
    )
    proj_low = proj_out.astype(bf16)
    proj_low_ref[...] = proj_low
    logits = forward_dot(proj_low, out_w_ref[...]) + out_b_ref[...]
    top = jnp.max(logits, axis=1, keepdims=True)
    powers = jnp.exp(logits - top)
    total = jnp.sum(powers, axis=1, keepdims=True)
    target = lax.broadcasted_iota(jnp.int32, (rows, vocab), 1) == label_ref[...]
    picked = jnp.sum(jnp.where(target, logits, 0.0), axis=1, keepdims=True)
    mask = mask_ref[...]
    loss_ref[...] = jnp.broadcast_to((jnp.log(total) + top - picked) * mask, (rows, LANES))
    logit_grad = (powers / total - target.astype(f32)) * mask
    out_b_grad_ref[...] = jnp.sum(logit_grad, axis=0, keepdims=True)
    logit_low = logit_grad.astype(bf16)
    logit_low_ref[...] = logit_low
    proj_grad = dot_last(logit_low, out_w_ref[...]) * (1.0 - proj_out * proj_out)
    proj_b_grad_ref[...] = jnp.sum(proj_grad, axis=0, keepdims=True)
    proj_grad_low = proj_grad.astype(bf16)
    proj_grad_ref[...] = proj_grad_low
    state_grad_ref[...] = dot_last(proj_grad_low, proj_ref[:hidden, :])
    context_grad_ref[...] = dot_last(proj_grad_low, proj_ref[hidden:, :]).astype(bf16)


def head(states, context, label_column, mask_column, proj_w, proj_b, out_w, out_b):
    rows, hidden = states.shape
    units = proj_w.shape[1]
    vocab = out_w.shape[1]
    return pl.pallas_call(
        head_kernel,
        in_specs=whole(8, False),
        out_shape=[
            jax.ShapeDtypeStruct((rows, LANES), f32),
            jax.ShapeDtypeStruct((1, vocab), f32),
            jax.ShapeDtypeStruct((1, units), f32),
            jax.ShapeDtypeStruct((rows, units), bf16),
            jax.ShapeDtypeStruct((rows, vocab), bf16),
            jax.ShapeDtypeStruct((rows, units), bf16),
            jax.ShapeDtypeStruct((rows, hidden), f32),
            jax.ShapeDtypeStruct((rows, hidden), bf16),
        ],
        compiler_params=params(),
        name="head",
    )(states, context, label_column, mask_column, proj_w, proj_b, out_w, out_b)


def swap(value):
    return lax.ppermute(value, "core", [(0, 1), (1, 0)])


def to_core(value, core):
    return lax.ppermute(value, "core", [(1 - core, core)])


def gather_columns(shard):
    return lax.all_gather(shard, ALL, axis=1, tiled=True)


def local(
    frames,
    noise,
    frame_lengths,
    labels,
    label_lengths,
    w_in,
    w_rec,
    ln_gain,
    ln_shift,
    init_state,
    dec_table,
    dec_rec,
    att_query,
    att_key,
    att_bias,
    att_vec,
    monotonic,
    proj_w,
    proj_b,
    out_w,
    out_b,
):
    core, chip, plane = (lax.axis_index("core"), lax.axis_index("chip"), lax.axis_index("batch"))
    planes, plane_chips = (lax.axis_size("batch"), lax.axis_size("chip"))
    chips = planes * plane_chips
    line = 2 * plane_chips
    utterances, slice_frames, feat = frames.shape
    label_steps = labels.shape[1]
    hidden = w_rec.shape[0]
    width = 4 * hidden
    vocab = out_b.shape[0]
    sharers = line // utterances
    chip_sharers = sharers // 2
    own_steps = label_steps // sharers
    utterance = chip // chip_sharers
    part = chip % chip_sharers
    share = part * 2 + core
    all_frames = line * slice_frames
    enc_frames = all_frames // chip_sharers
    on_enc = core == 0
    core_arg = core.astype(jnp.int32).reshape(1)
    gain_row, shift_row = (ln_gain.reshape(1, -1), ln_shift.reshape(1, -1))

    all_labels = lax.all_gather(labels, "batch", axis=0, tiled=True)
    prev_ids = jnp.concatenate(
        [jnp.zeros((planes * utterances, 1), jnp.int32), all_labels[:, :-1]], axis=1
    )
    onehot = (prev_ids.reshape(-1)[:, None] == jnp.arange(vocab)[None, :]).astype(bf16)
    rows_here = forward_dot(onehot, dec_table).astype(bf16).reshape(planes * utterances, label_steps, -1)
    rows_here = jnp.repeat(rows_here, chip_sharers, axis=0)
    rows_mine = lax.all_to_all(rows_here, CHIPS, 0, 0, tiled=True)
    rows_other = swap(rows_mine)
    low_rows = jnp.where(on_enc, rows_mine, rows_other)
    high_rows = jnp.where(on_enc, rows_other, rows_mine)
    table_rows = jnp.stack([low_rows, high_rows], axis=1)
    table_rows = table_rows.transpose(2, 0, 1, 3).reshape(label_steps, width).astype(f32)

    full_dec = gather_columns(dec_rec)
    states_dec, dec_gates, dec_cells = dec_forward(core_arg, table_rows, full_dec)

    if chip_sharers == 1:
        pieces = frames.reshape(utterances, slice_frames, feat)
        pieces = pieces.reshape(utterances, 2, slice_frames // 2, feat).reshape(line, slice_frames // 2, feat)
        got = lax.all_to_all(pieces, ("chip", "core"), 0, 0, tiled=True)
        other = to_core(got, 0)
        enc_in = jnp.stack([got, other], axis=1).reshape(enc_frames, feat)
    else:
        got = lax.all_gather(frames, ("chip", "core"), axis=0)
        got = lax.dynamic_index_in_dim(got, utterance, 1, keepdims=False).reshape(all_frames, feat)
        enc_in = lax.dynamic_slice_in_dim(got, part * enc_frames, enc_frames, axis=0)
    enc_rows = enc_frames // BLOCK
    frame_rows = enc_in.reshape(enc_rows, BLOCK, feat).transpose(1, 0, 2).reshape(enc_frames, feat)
    noise_pieces = noise.reshape(line, own_steps, slice_frames)
    noise_own = lax.all_to_all(noise_pieces, ("chip", "core"), 0, 0, tiled=True)
    noise_own = noise_own.transpose(1, 0, 2).reshape(own_steps, all_frames)

    full_in, full_rec = (gather_columns(w_in), gather_columns(w_rec))
    enc_hidden, enc_norm, enc_cell, enc_scale = enc_forward(
        core_arg, frame_rows, full_in, full_rec, gain_row, shift_row, init_state
    )
    memory_part = enc_hidden.transpose(1, 0, 2).reshape(enc_frames, hidden)
    memory = jnp.where(on_enc, memory_part, to_core(memory_part, 1))
    if chip_sharers > 1:
        groups = [
            [first * chip_sharers + i for i in range(chip_sharers)] for first in range(utterances)
        ]
        memory = lax.all_gather(memory, "chip", axis=0, tiled=True, axis_index_groups=groups)

    full_query, full_key = (gather_columns(att_query), gather_columns(att_key))
    full_proj = gather_columns(proj_w)
    full_out = lax.all_gather(out_w, ALL, axis=0, tiled=True)

    states_low = states_dec.astype(bf16)
    states_all = jnp.where(on_enc, to_core(states_low, 0), states_low)
    states_own = lax.dynamic_slice_in_dim(states_all, share * own_steps, own_steps, axis=0)
    queries = forward_dot(states_own, full_query) + att_bias.reshape(1, -1)
    keys = forward_dot(memory, full_key)

    norm_inv = lax.rsqrt(jnp.sum(att_vec[0] * att_vec[0]) + 1e-06)
    scalars = jnp.stack([monotonic[0] * norm_inv, monotonic[1]])
    length = lax.dynamic_slice_in_dim(frame_lengths, utterance, 1)
    attended = attend(scalars, length, queries, keys, att_vec, noise_own, memory)
    saved, weight_low, context = (attended[:5], attended[5], attended[6])

    label_row = lax.dynamic_slice(labels, (utterance, share * own_steps), (1, own_steps))
    label_length = lax.dynamic_slice_in_dim(label_lengths, utterance, 1)
    step_ids = share * own_steps + jnp.arange(own_steps)
    mask_column = (step_ids < label_length).astype(f32).reshape(own_steps, 1)
    loss_rows, out_b_grad, proj_b_grad, proj_low, logit_low, proj_grad_low, state_head, context_grad = head(
        states_own,
        context,
        label_row.reshape(own_steps, 1),
        mask_column,
        full_proj,
        proj_b.reshape(1, -1),
        full_out,
        out_b.reshape(1, -1),
    )

    key_low, query_grad, vec_raw, mono_parts = attend_back(
        scalars, length, context_grad, memory, saved, queries, keys, att_vec
    )
    query_low = query_grad.astype(bf16)
    bias_grad = jnp.sum(query_grad, axis=0).reshape(2, -1)
    gain_part = mono_parts[0, 0]
    vec_fix = -gain_part * monotonic[0] * norm_inv * norm_inv * norm_inv
    vec_grad = vec_raw.at[0].add(vec_fix * att_vec[0])
    mono_grad = jnp.stack([gain_part * norm_inv, mono_parts[0, 1]])

    memory_grad = dot_first(weight_low, context_grad) + dot_last(key_low, full_key)
    att_key_part = dot_first(memory, key_low).astype(bf16)
    if chip_sharers > 1:
        memory_grad = lax.psum_scatter(
            memory_grad, "chip", scatter_dimension=0, tiled=True, axis_index_groups=groups
        )
    memory_grad = memory_grad + to_core(memory_grad.astype(bf16), 0).astype(f32)
    memory_steps = memory_grad.reshape(enc_rows, BLOCK, hidden).transpose(1, 0, 2)

    state_grad = state_head + dot_last(query_low, full_query)
    both = jnp.stack([to_core(state_grad, 1), state_grad]).reshape(2 * own_steps, hidden)
    if chip_sharers > 1:
        both = lax.all_gather(both, "chip", axis=0, tiled=True, axis_index_groups=groups)

    enc_grad, gain_grad, shift_grad, init_grad = enc_backward(
        core_arg, enc_norm, enc_cell, enc_scale, memory_steps, full_rec, gain_row, shift_row, init_state
    )
    dec_grad = dec_backward(core_arg, dec_gates, dec_cells, both, full_dec)

    enc_grad_rows = enc_grad.reshape(enc_frames, width)
    start_hidden = jnp.broadcast_to(init_state[0].astype(bf16), (1, enc_rows, hidden))
    prev_hidden = jnp.concatenate([start_hidden, enc_hidden[:-1]], axis=0).reshape(enc_frames, hidden)
    rec_part = dot_first(prev_hidden, enc_grad_rows).astype(bf16)
    in_part = dot_first(frame_rows, enc_grad_rows).astype(bf16)
    w_rec_out = lax.psum_scatter(rec_part, ALL, scatter_dimension=1, tiled=True).astype(f32)
    w_in_out = lax.psum_scatter(in_part, ALL, scatter_dimension=1, tiled=True).astype(f32)
    key_out = lax.psum_scatter(att_key_part, ALL, scatter_dimension=1, tiled=True).astype(f32)

    frames_part = dot_last(enc_grad_rows, full_in).astype(bf16)
    frames_part = frames_part.reshape(BLOCK, enc_rows, feat).transpose(1, 0, 2).reshape(enc_frames, feat)
    if chip_sharers == 1:
        halves = frames_part.reshape(line, 2, slice_frames // 2, feat)
        mine = jnp.where(on_enc, halves[:, 0], to_core(halves[:, 1], 1))
        back = lax.all_to_all(mine, ("chip", "core"), 0, 0, tiled=True)
        frames_grad = back.reshape(utterances, slice_frames, feat).astype(f32)
    else:
        everyone = lax.all_gather(frames_part, ("chip", "core"), axis=0)
        everyone = everyone.reshape(utterances, chip_sharers, 2, enc_frames, feat)[:, :, 0]
        everyone = everyone.reshape(utterances, all_frames, feat)
        at = (chip * 2 + core) * slice_frames
        frames_grad = lax.dynamic_slice_in_dim(everyone, at, slice_frames, axis=1).astype(f32)

    row_parts = jnp.concatenate([states_own, context, logit_low], axis=1)
    row_all = lax.all_gather(row_parts, ALL, axis=0, tiled=True)
    rows_total = row_all.shape[0]
    states_rows = row_all[:, :hidden]
    joined_rows = row_all[:, : 2 * hidden]
    logit_rows = row_all[:, 2 * hidden :]
    by_utt = states_rows.reshape(planes * utterances, label_steps, hidden)
    states_prev = jnp.concatenate([jnp.zeros_like(by_utt[:, :1]), by_utt[:, :-1]], axis=1)
    states_prev = states_prev.reshape(rows_total, hidden)

    def for_chips(value):
        pair = jnp.concatenate([value, to_core(value, 0)], axis=0)
        return pair.reshape(2 * own_steps, chips, -1).transpose(1, 0, 2)

    head_pack = jnp.concatenate(
        [for_chips(query_low), for_chips(proj_grad_low), for_chips(proj_low)], axis=2
    )
    dec_own = lax.dynamic_slice_in_dim(dec_grad, part * 2 * own_steps, 2 * own_steps, axis=0)
    dec_pack = dec_own.astype(bf16).reshape(2 * own_steps, chips, -1).transpose(1, 0, 2)
    pack = lax.all_to_all(jnp.where(on_enc, head_pack, dec_pack), CHIPS, 0, 0, tiled=True)
    pack = pack.reshape(rows_total, -1)
    query_cols = 2 * att_query.shape[1]
    proj_cols = 2 * proj_w.shape[1]
    query_pair = dot_first(states_rows, pack[:, :query_cols])
    proj_pair = dot_first(joined_rows, pack[:, query_cols : query_cols + proj_cols])
    out_pair = dot_first(pack[:, query_cols + proj_cols :], logit_rows)
    rec_pair = dot_first(states_prev, pack)
    table_pair = dot_first(onehot, pack)

    def settle(pair, axis, owner):
        low, high = jnp.split(pair, 2, axis=axis)
        if owner == 0:
            return jnp.where(on_enc, low, to_core(high, 1))
        return jnp.where(on_enc, to_core(low, 0), high)

    query_out = settle(query_pair, 1, 0)
    proj_w_out = settle(proj_pair, 1, 0)
    out_w_out = settle(out_pair, 0, 0)
    dec_rec_out = settle(rec_pair, 1, 1)
    table_out = settle(table_pair, 1, 1)

    loss_out, init_out, gain_out, shift_out, bias_out, vec_out, mono_out, proj_b_out, out_b_out = lax.psum(
        (
            jnp.sum(loss_rows[:, 0]),
            init_grad,
            gain_grad.reshape(-1),
            shift_grad.reshape(-1),
            bias_grad,
            vec_grad,
            mono_grad,
            proj_b_grad.reshape(-1),
            out_b_grad.reshape(-1),
        ),
        ALL,
    )
    return (
        loss_out,
        frames_grad,
        w_in_out,
        w_rec_out,
        gain_out,
        shift_out,
        init_out,
        table_out,
        dec_rec_out,
        query_out,
        key_out,
        bias_out,
        vec_out,
        mono_out,
        proj_w_out,
        proj_b_out,
        out_w_out,
        out_b_out,
    )


def solution(mesh):
    planes, line = mesh.devices.shape
    fine = Mesh(mesh.devices.reshape(planes, line // 2, 2), ALL)
    tm = ("chip", "core")
    columns = P(None, ALL)
    return jax.shard_map(
        local,
        mesh=fine,
        in_specs=(
            P("batch", tm, None),
            P("batch", None, tm),
            P("batch"),
            P("batch", None),
            P("batch"),
            columns,
            columns,
            P(),
            P(),
            P(),
            columns,
            columns,
            columns,
            columns,
            P(),
            P(),
            P(),
            columns,
            P(),
            P(ALL, None),
            P(),
        ),
        out_specs=(
            P(),
            P("batch", tm, None),
            columns,
            columns,
            P(),
            P(),
            P(),
            columns,
            columns,
            columns,
            columns,
            P(),
            P(),
            P(),
            columns,
            P(),
            P(ALL, None),
            P(),
        ),
        check_vma=False,
    )
```
